256 devices in a mesh: dp: 16 (over z_hi, x, core), mp: 16 (over z_lo, y).
Axes of the slice: x: 4, y: 4, z: 8 (z_hi: 2, z_lo: 4; z = z_hi * 4 + z_lo), core: 2. Of those that a mesh axis runs over, the one named last changes fastest.
Arguments:
- tokens: bfloat16 [8192, 3072], P(('dp', 'mp')), may hold values from -500 to 500
- gain: float32 [3072], replicated, may hold values from 0.5 to 1.5
- encoder: bfloat16 [3072, 384], P('dp'), may hold values from -0.109375 to 0.109375
- w_up: bfloat16 [3072, 12288], P(None, 'mp'), may hold values from -0.3125 to 0.3125
- w_down: bfloat16 [3072, 12288], P(None, 'mp'), may hold values from -0.0546875 to 0.0546875
- cotangent: bfloat16 [8192, 3072], P(('dp', 'mp')), may hold values from -6 to 6
Outputs:
- grad_tokens: bfloat16 [8192, 3072], P(('dp', 'mp'))
- grad_up: float32 [3072, 12288], P('dp', 'mp')
- grad_down: float32 [3072, 12288], P('dp', 'mp')
- grad_encoder: float32 [3072, 384], P(('dp', 'mp'))
- grad_gain: float32 [3072], P(('dp', 'mp'))
The draws below stay inside these ranges and needn't reach their ends.
All inputs are finite; a program needn't handle non-finite values.
Results may differ from the reference program's by a relative error of at most 0.035.
Values may be sent and summed in bfloat16 or wider, within the bound.
No kernel may reach another device: no remote copies, remote signals or barrier semaphores. Data moves between devices by JAX's collectives and lax.ppermute only.
A program may use at most 128 MiB of HBM per device.

```python
import math
import jax
import jax.numpy as jnp
from jax import lax

D = 3072
FF = 12288
COMP = 384
GROUP = 512
TOKENS = 8192
FF_DEV = 768
N_DP = 16
N_MP = 16


def draw_tokens(key, part):
    key = jax.random.fold_in(key, 11)
    k_base, k_rows, k_cols = jax.random.split(key, 3)
    row_scale = jnp.exp(jax.random.uniform(k_rows, (TOKENS, 1), jnp.float32, 0.0, math.log(10.0)))
    col_scale = jnp.exp(jax.random.uniform(k_cols, (1, D), jnp.float32, 0.0, math.log(10.0)))
    base = jnp.clip(jax.random.normal(k_base, (TOKENS, D), jnp.float32), -5.0, 5.0)
    return (base * row_scale * col_scale).astype(jnp.bfloat16)


def with_spikes(drawn, own_key, source, target, shards_of, factor):
    owner, partner = [(jnp.arange(drawn.shape[axis_at]) // (drawn.shape[axis_at] // shards_of)).reshape([-1 if axis == axis_at else 1 for axis in range(drawn.ndim)]) for axis_at in (source, target)]
    chosen = jax.random.permutation(own_key, shards_of)[partner]
    strong = (owner == chosen) | (owner == (partner + shards_of // 2) % shards_of)
    return jnp.where(strong, factor * drawn, drawn)


def block_levels(stream_key, extent, pieces, smallest, high):
    factor_of = 1.0
    for axis_at, parts in pieces:
        heights = jax.random.uniform(jax.random.fold_in(jax.random.fold_in(stream_key, 6), axis_at), (parts,), jnp.float32, smallest / len(pieces), high / len(pieces))
        factor_of = factor_of * jnp.repeat(jnp.exp(heights), extent[axis_at] // parts).reshape((-1,) + (1,) * (len(extent) - 1 - axis_at))
    return factor_of


def normal_values(key, shape, spread, most, pieces=(), kind=jnp.bfloat16):
    array = jax.random.normal(key, shape, jnp.float32) * spread
    if len(pieces) > 0:
        array = block_levels(key, shape, pieces, -0.22, 0.18) * array
    return jnp.clip(array, min=-most, max=most).astype(kind)


def bell_draw_with(stream_key, extent, deviation, bound, shards, heavy, held_as=jnp.bfloat16):
    result = deviation * jax.random.normal(stream_key, extent, jnp.float32)
    if shards:
        result = result * block_levels(stream_key, extent, shards, -0.22, 0.18)
    return jnp.clip(with_spikes(result, jax.random.fold_in(stream_key, 3), *heavy), -bound, bound).astype(held_as)


def setup_inputs(seed: int = 0) -> dict:
    key_list = jax.random.split(jax.random.key(seed), 7)
    tokens = draw_tokens(jax.random.fold_in(key_list[6], 71), 0)
    gain = jnp.clip(1.0 + 0.1 * jax.random.normal(key_list[1], (D,), jnp.float32), 0.5, 1.5)
    encoder = normal_values(key_list[2], (D, COMP), D ** -0.5, 0.109375, ((0, 16),))
    w_up = normal_values(key_list[3], (D, FF), COMP ** -0.5, 0.3125, ((1, 16),))
    w_down = normal_values(key_list[4], (D, FF), FF ** -0.5, 0.0546875, ((1, 16),))
    cotangent = bell_draw_with(key_list[5], (TOKENS, D), 0.25, 6.0, ((0, 256),), (0, 1, 256, 6.0))
    return dict(tokens=tokens, gain=gain, encoder=encoder, w_up=w_up, w_down=w_down, cotangent=cotangent)


def gelu_parts(pre_act):
    cdf_part = 0.5 * (1.0 + lax.erf(pre_act * 0.7071067811865476))
    density = jnp.exp(-0.5 * pre_act * pre_act) * 0.3989422804014327
    return (pre_act * cdf_part, cdf_part + pre_act * density)

def sum_rounded(terms):
    rounded = lax.optimization_barrier(terms.astype(jnp.bfloat16))
    return lax.optimization_barrier(jnp.sum(rounded.astype(jnp.float32), axis=0))

def reference(tokens, gain, encoder, w_up, w_down, cotangent):
    as_float = tokens.astype(jnp.float32)
    center = as_float - lax.optimization_barrier(jnp.mean(as_float, axis=1, keepdims=True))
    inv_std = lax.rsqrt(lax.optimization_barrier(jnp.mean(center * center, axis=1, keepdims=True)) + 1e-06)
    unit = center * inv_std
    normed = (unit * gain).astype(jnp.bfloat16)
    code_rows = jnp.dot(normed, encoder, preferred_element_type=jnp.float32).astype(jnp.bfloat16)
    decoded = jnp.dot(code_rows, encoder.T, preferred_element_type=jnp.float32).astype(jnp.bfloat16)
    up_blocks = w_up.reshape(D, N_MP, FF_DEV).transpose(1, 0, 2)
    down_blocks = w_down.reshape(D, N_MP, FF_DEV).transpose(1, 0, 2)
    grouped_dec = decoded.reshape(N_DP, GROUP, D).astype(jnp.float32)
    grouped_cot = cotangent.reshape(N_DP, GROUP, D).astype(jnp.float32)

    def one_block(running, weights):
        up_part, down_part = weights
        pre_act = jnp.dot(decoded, up_part, preferred_element_type=jnp.float32)
        gelu_val, gelu_slope = gelu_parts(pre_act)
        hidden = gelu_val.astype(jnp.bfloat16)
        d_act = (jnp.dot(cotangent, down_part, preferred_element_type=jnp.float32) * gelu_slope).astype(jnp.bfloat16)
        partial_value = jnp.dot(d_act, up_part.T, preferred_element_type=jnp.float32).astype(jnp.bfloat16)
        grouped_act = d_act.reshape(N_DP, GROUP, FF_DEV).astype(jnp.float32)
        grouped_hid = hidden.reshape(N_DP, GROUP, FF_DEV).astype(jnp.float32)
        up_grad = sum_rounded(jnp.einsum('gtd,gtf->gdf', grouped_dec, grouped_act))
        down_grad = sum_rounded(jnp.einsum('gtd,gtf->gdf', grouped_cot, grouped_hid))
        return (running + partial_value.astype(jnp.float32), (up_grad, down_grad))
    summed, (up_parts, down_parts) = lax.scan(one_block, jnp.zeros((TOKENS, D), jnp.float32), (up_blocks, down_blocks))
    grad_up = up_parts.transpose(1, 0, 2).reshape(D, FF)
    grad_down = down_parts.transpose(1, 0, 2).reshape(D, FF)
    grad_codes = jnp.dot(summed, encoder.astype(jnp.float32), precision=lax.Precision.HIGHEST).astype(jnp.bfloat16)
    decode_term = jnp.dot(summed.T, code_rows.astype(jnp.float32), precision=lax.Precision.HIGHEST)
    encode_term = jnp.dot(normed.T, grad_codes, preferred_element_type=jnp.float32)
    d_normed = jnp.dot(grad_codes, encoder.T, preferred_element_type=jnp.float32)
    grad_gain = lax.optimization_barrier(jnp.sum(d_normed * unit, axis=0))
    dx_hat = d_normed * gain
    mean_one = lax.optimization_barrier(jnp.mean(dx_hat, axis=1, keepdims=True))
    mean_two = lax.optimization_barrier(jnp.mean(dx_hat * unit, axis=1, keepdims=True))
    grad_tokens = (cotangent.astype(jnp.float32) + inv_std * (dx_hat - mean_one - unit * mean_two)).astype(jnp.bfloat16)
    return (grad_tokens, grad_up, grad_down, encode_term + decode_term, grad_gain)
```

```python
import jax
import jax.numpy as jnp
from jax import lax
from jax.sharding import PartitionSpec as P

F32 = jnp.float32
BF16 = jnp.bfloat16


def gelu_parts(pre_act):
    cdf_part = 0.5 * (1.0 + lax.erf(pre_act * 0.7071067811865476))
    density = jnp.exp(-0.5 * pre_act * pre_act) * 0.3989422804014327
    return (pre_act * cdf_part, cdf_part + pre_act * density)


def on_device(tokens, gain, encoder, w_up, w_down, cotangent):
    rows = encoder.shape[0]
    own = rows // lax.axis_size("mp")
    dp_at = lax.axis_index("dp")
    mp_at = lax.axis_index("mp")
    full_encoder = lax.all_gather(encoder, "dp", axis=0, tiled=True)
    as_float = tokens.astype(F32)
    center = as_float - jnp.mean(as_float, axis=1, keepdims=True)
    inv_std = lax.rsqrt(jnp.mean(center * center, axis=1, keepdims=True) + 1e-06)
    unit = center * inv_std
    normed = (unit * gain).astype(BF16)
    code_rows = jnp.dot(normed, full_encoder, preferred_element_type=F32).astype(BF16)
    all_codes = lax.all_gather(code_rows, "mp", axis=0, tiled=True)
    tied_up = jnp.einsum("dc,df->cf", full_encoder, w_up, preferred_element_type=F32).astype(BF16)
    pre_act = jnp.dot(all_codes, tied_up, preferred_element_type=F32)
    gelu_val, gelu_slope = gelu_parts(pre_act)
    hidden = gelu_val.astype(BF16)
    upstream = lax.all_gather(cotangent, "mp", axis=0, tiled=True)
    d_hidden = jnp.dot(upstream, w_down, preferred_element_type=F32)
    d_act = (d_hidden * gelu_slope).astype(BF16)
    down_term = jnp.einsum("td,tf->df", upstream, hidden, preferred_element_type=F32)
    grad_down = lax.psum_scatter(
        down_term.astype(BF16), "dp", scatter_dimension=0, tiled=True
    ).astype(F32)
    codes_part = jnp.einsum("tf,cf->tc", d_act, tied_up, preferred_element_type=F32)
    grad_codes = lax.psum_scatter(codes_part, "mp", scatter_dimension=0, tiled=True).astype(BF16)
    inner = jnp.einsum("tc,tf->cf", all_codes, d_act, preferred_element_type=F32)
    inner = lax.psum(inner, "dp").astype(BF16)
    grad_up = jnp.dot(encoder, inner, preferred_element_type=F32)
    up_rows = lax.dynamic_slice_in_dim(w_up, dp_at * rows, rows, 0)
    decode_part = jnp.einsum("df,cf->dc", up_rows, inner, preferred_element_type=F32)
    unit_cols = lax.all_to_all(unit.astype(BF16), "dp", split_axis=1, concat_axis=0, tiled=True)
    codes_cols = lax.all_gather(grad_codes, "dp", axis=0, tiled=True)
    encode_part = jnp.einsum("td,tc->dc", unit_cols, codes_cols, preferred_element_type=F32)
    both = lax.psum_scatter(
        jnp.concatenate([encode_part, decode_part], axis=1), "mp", scatter_dimension=0, tiled=True
    )
    width = encoder.shape[1]
    own_encoder = lax.dynamic_slice_in_dim(encoder, mp_at * own, own, 0).astype(F32)
    own_gain = lax.dynamic_slice_in_dim(gain, dp_at * rows + mp_at * own, own, 0)
    grad_encoder = own_gain[:, None] * both[:, :width] + both[:, width:]
    grad_gain = jnp.sum(own_encoder * both[:, :width], axis=1)
    d_normed = jnp.einsum("tc,dc->td", grad_codes, full_encoder, preferred_element_type=F32)
    dx_hat = d_normed * gain
    mean_one = jnp.mean(dx_hat, axis=1, keepdims=True)
    mean_two = jnp.mean(dx_hat * unit, axis=1, keepdims=True)
    grad_tokens = (
        cotangent.astype(F32) + inv_std * (dx_hat - mean_one - unit * mean_two)
    ).astype(BF16)
    return (grad_tokens, grad_up, grad_down, grad_encoder, grad_gain)


def solution(mesh):
    placed = (
        P(("dp", "mp"), None),
        P(),
        P("dp", None),
        P(None, "mp"),
        P(None, "mp"),
        P(("dp", "mp"), None),
    )
    return jax.shard_map(
        on_device,
        mesh=mesh,
        in_specs=placed,
        out_specs=(
            P(("dp", "mp"), None),
            P("dp", "mp"),
            P("dp", "mp"),
            P(("dp", "mp"), None),
            P(("dp", "mp")),
        ),
        check_vma=False,
    )
```

```python
import jax
import jax.numpy as jnp
from jax import lax
from jax.sharding import PartitionSpec as P

F32 = jnp.float32
BF16 = jnp.bfloat16
CHUNKS = 2


def step_core(i):
    return i ^ 1


def step_far(i):
    return i ^ 8


def step_x(k):
    return lambda i: (i & 9) | ((((i >> 1) + k) & 3) << 1)


def step_y(k):
    return lambda i: (i & 12) | ((i + k) & 3)


def step_z(k):
    return lambda i: ((((i >> 2) + k) & 3) << 2) | (i & 3)


def send(value, axis, target):
    return lax.ppermute(value, axis, [(i, target(i)) for i in range(16)])


def gather_parts(value, axis, step):
    return [value] + [send(value, axis, step(-k)) for k in (1, 2, 3)]


def in_order(parts, at):
    n = len(parts)
    twice = jnp.stack(parts + parts[:-1])
    return lax.dynamic_slice_in_dim(twice, (n - at) % n, n, 0)


def pair_in_order(mine, other, at):
    first = jnp.where(at == 0, mine, other)
    second = jnp.where(at == 0, other, mine)
    return first, second


def pick(value, at, axis):
    return lax.dynamic_index_in_dim(value, at, axis, keepdims=False)


def gelu_parts(pre_act):
    cdf_part = 0.5 * (1.0 + lax.erf(pre_act * 0.7071067811865476))
    density = jnp.exp(-0.5 * pre_act * pre_act) * 0.3989422804014327
    return (pre_act * cdf_part, cdf_part + pre_act * density)


def add(a, b):
    return a.astype(F32) + b.astype(F32)


def gather_encoder(encoder, x, core, far):
    rows, width = encoder.shape
    other = send(encoder, "dp", step_far)
    both = jnp.stack(pair_in_order(encoder, other, far))
    along = in_order(gather_parts(both, "dp", step_x), x)
    across = send(along, "dp", step_core)
    full = jnp.stack(pair_in_order(along, across, core), axis=2)
    return full.transpose(1, 0, 2, 3, 4).reshape(16 * rows, width)


def gather_cotangent(cotangent):
    line = jnp.concatenate(gather_parts(cotangent, "mp", step_z), axis=0)
    half = line.shape[0] // 2
    after = send(line, "mp", step_y(-1))
    before = send(line, "mp", step_y(1))
    far_a = send(after[:half], "mp", step_y(-1))
    far_b = send(before[half:], "mp", step_y(1))
    return jnp.concatenate([line, after, far_a, far_b, before], axis=0)


def gather_codes(code_rows):
    line = jnp.concatenate(gather_parts(code_rows, "mp", step_z), axis=0)
    return jnp.concatenate(gather_parts(line, "mp", step_y), axis=0)


def scatter_codes(part):
    for step in (step_y, step_z):
        blocks = part.reshape(4, -1, part.shape[1])
        sent = [send(blocks[k].astype(BF16), "mp", step(k)) for k in (1, 2, 3)]
        part = blocks[0] + sum(s.astype(F32) for s in sent)
    return part


def reduce_inner(inner, x, core):
    rows, cols = inner.shape
    halves = inner.astype(BF16).reshape(2, rows // 2, cols)
    part = add(pick(halves, core, 0), send(pick(halves, 1 - core, 0), "dp", step_core))
    quarters = part.astype(BF16).reshape(4, rows // 8, cols)
    total = pick(quarters, x, 0).astype(F32)
    for k in (1, 2, 3):
        total = total + send(pick(quarters, (x + k) % 4, 0), "dp", step_x(k)).astype(F32)
    total = total.astype(BF16)
    total = add(total, send(total, "dp", step_far)).astype(BF16)
    half = in_order(gather_parts(total, "dp", step_x), x).reshape(rows // 2, cols)
    other = send(half, "dp", step_core)
    return jnp.concatenate(pair_in_order(half, other, core), axis=0)


def scatter_term(term, x, core, far):
    rows = term.shape[0] // 16
    cols = term.shape[1]
    by_core = term.reshape(8, 2, rows, cols)
    summed = add(pick(by_core, core, 1), send(pick(by_core, 1 - core, 1), "dp", step_core))
    summed = summed.astype(BF16).reshape(2, 4, rows, cols)
    chunk = [pick(summed, (x + k) % 4, 1) for k in range(4)]
    half = rows // 2
    got_a = send(chunk[2][:, :half], "dp", step_x(1))
    got_b = send(chunk[2][:, half:], "dp", step_x(-1))
    up = jnp.concatenate(
        [add(chunk[1][:, :half], got_a).astype(BF16), chunk[1][:, half:]], axis=1
    )
    down = jnp.concatenate(
        [chunk[3][:, :half], add(chunk[3][:, half:], got_b).astype(BF16)], axis=1
    )
    total = add(chunk[0], send(up, "dp", step_x(1))) + send(down, "dp", step_x(-1)).astype(F32)
    other = send(pick(total, 1 - far, 0).astype(BF16), "dp", step_far)
    return pick(total, far, 0) + other.astype(F32)


def on_device(tokens, gain, encoder, w_up, w_down, cotangent):
    rows, width = encoder.shape
    own = rows // 16
    dp_at = lax.axis_index("dp")
    mp_at = lax.axis_index("mp")
    core, x, far = dp_at % 2, (dp_at // 2) % 4, dp_at // 8

    full_encoder = gather_encoder(encoder, x, core, far)
    upstream = gather_cotangent(cotangent)
    as_float = tokens.astype(F32)
    center = as_float - jnp.mean(as_float, axis=1, keepdims=True)
    inv_std = lax.rsqrt(jnp.mean(center * center, axis=1, keepdims=True) + 1e-06)
    unit = center * inv_std
    normed = (unit * gain).astype(BF16)
    code_rows = jnp.dot(normed, full_encoder, preferred_element_type=F32).astype(BF16)
    all_codes = gather_codes(code_rows)
    tied_up = jnp.einsum("dc,df->cf", full_encoder, w_up, preferred_element_type=F32).astype(BF16)
    pre_act = jnp.dot(all_codes, tied_up, preferred_element_type=F32)
    gelu_val, gelu_slope = gelu_parts(pre_act)
    hidden = gelu_val.astype(BF16)
    d_hidden = jnp.dot(upstream, w_down, preferred_element_type=F32)
    d_act = (d_hidden * gelu_slope).astype(BF16)
    codes_part = jnp.einsum("tf,cf->tc", d_act, tied_up, preferred_element_type=F32)
    grad_codes = scatter_codes(codes_part).astype(BF16)
    inner = jnp.einsum("tc,tf->cf", all_codes, d_act, preferred_element_type=F32)
    inner = reduce_inner(inner, x, core)
    span = hidden.shape[1] // CHUNKS
    down_parts = []
    for at in range(CHUNKS):
        cut = hidden[:, at * span : (at + 1) * span]
        term = jnp.einsum("td,tf->df", upstream, cut, preferred_element_type=F32)
        down_parts.append(scatter_term(term.astype(BF16), x, core, far))
    grad_down = jnp.concatenate(down_parts, axis=1)
    grad_up = jnp.dot(encoder, inner, preferred_element_type=F32)
    up_rows = lax.dynamic_slice_in_dim(w_up, dp_at * rows, rows, 0)
    decode_part = jnp.einsum("df,cf->dc", up_rows, inner, preferred_element_type=F32)
    unit_cols = lax.all_to_all(unit.astype(BF16), "dp", split_axis=1, concat_axis=0, tiled=True)
    codes_cols = lax.all_to_all(
        jnp.broadcast_to(grad_codes, (16,) + grad_codes.shape), "dp", split_axis=0, concat_axis=0
    ).reshape(unit_cols.shape[0], width)
    encode_part = jnp.einsum("td,tc->dc", unit_cols, codes_cols, preferred_element_type=F32)
    both = jnp.concatenate([encode_part, decode_part], axis=1).astype(BF16)
    both = lax.all_to_all(both.reshape(16, own, 2 * width), "mp", split_axis=0, concat_axis=0)
    both = jnp.sum(both.astype(F32), axis=0)
    own_encoder = lax.dynamic_slice_in_dim(encoder, mp_at * own, own, 0).astype(F32)
    own_gain = lax.dynamic_slice_in_dim(gain, dp_at * rows + mp_at * own, own, 0)
    grad_encoder = own_gain[:, None] * both[:, :width] + both[:, width:]
    grad_gain = jnp.sum(own_encoder * both[:, :width], axis=1)
    d_normed = jnp.einsum("tc,dc->td", grad_codes, full_encoder, preferred_element_type=F32)
    dx_hat = d_normed * gain
    mean_one = jnp.mean(dx_hat, axis=1, keepdims=True)
    mean_two = jnp.mean(dx_hat * unit, axis=1, keepdims=True)
    grad_tokens = (
        cotangent.astype(F32) + inv_std * (dx_hat - mean_one - unit * mean_two)
    ).astype(BF16)
    return (grad_tokens, grad_up, grad_down, grad_encoder, grad_gain)


def solution(mesh):
    placed = (
        P(("dp", "mp"), None),
        P(),
        P("dp", None),
        P(None, "mp"),
        P(None, "mp"),
        P(("dp", "mp"), None),
    )
    return jax.shard_map(
        on_device,
        mesh=mesh,
        in_specs=placed,
        out_specs=(
            P(("dp", "mp"), None),
            P("dp", "mp"),
            P("dp", "mp"),
            P(("dp", "mp"), None),
            P(("dp", "mp")),
        ),
        check_vma=False,
    )
```

```python
import jax
import jax.numpy as jnp
from jax import lax
from jax.experimental import pallas as pl
from jax.experimental.pallas import tpu as pltpu
from jax.sharding import PartitionSpec as P

F32 = jnp.float32
BF16 = jnp.bfloat16


def step_core(i):
    return i ^ 1


def step_far(i):
    return i ^ 8


def step_x(k):
    return lambda i: (i & 9) | ((((i >> 1) + k) & 3) << 1)


def step_y(k):
    return lambda i: (i & 12) | ((i + k) & 3)


def step_z(k):
    return lambda i: ((((i >> 2) + k) & 3) << 2) | (i & 3)


def send(value, axis, target):
    return lax.ppermute(value, axis, [(i, target(i)) for i in range(16)])


def gather_parts(value, axis, step):
    return [value] + [send(value, axis, step(-k)) for k in (1, 2, 3)]


def in_order(parts, at):
    n = len(parts)
    twice = jnp.stack(parts + parts[:-1])
    return lax.dynamic_slice_in_dim(twice, (n - at) % n, n, 0)


def pair_in_order(mine, other, at):
    first = jnp.where(at == 0, mine, other)
    second = jnp.where(at == 0, other, mine)
    return first, second


def pick(value, at, axis):
    return lax.dynamic_index_in_dim(value, at, axis, keepdims=False)


def gelu_parts(pre_act):
    cdf_part = 0.5 * (1.0 + lax.erf(pre_act * 0.7071067811865476))
    density = jnp.exp(-0.5 * pre_act * pre_act) * 0.3989422804014327
    return (pre_act * cdf_part, cdf_part + pre_act * density)


def add(a, b):
    return a.astype(F32) + b.astype(F32)


def join_encoder(along, across, core):
    full = jnp.stack(pair_in_order(along, across, core), axis=2)
    return full.transpose(1, 0, 2, 3, 4).reshape(-1, along.shape[-1])


def gather_codes(code_rows):
    count, width = code_rows.shape
    return lax.all_to_all(
        jnp.broadcast_to(code_rows, (16, count, width)), "mp", split_axis=0, concat_axis=0
    )


def scatter_codes(part):
    got = lax.all_to_all(part, "mp", split_axis=0, concat_axis=0)
    return jnp.sum(got.astype(F32), axis=0)


STEPS = 6
VMEM = 20 * 1024 * 1024


def hidden_kernel(
    at, codes, tied, w_down, p0, p1, p2, p3, p4, hidden, codes_part, inner, rows, slope, total
):
    step = pl.program_id(0)
    z, y, core, x = at[0], at[1], at[2], at[3]
    count = codes.shape[1]

    def block(k):
        return ((z + k % 4) % 4) * 4 + (y + k // 4) % 4

    @pl.when(step == 0)
    def _():
        for k in range(16):
            rows[k * count : (k + 1) * count, :] = codes[block(k)]
        pre_act = jnp.dot(rows[...], tied[...], preferred_element_type=F32)
        value, grade = gelu_parts(pre_act)
        hidden[...] = value.astype(BF16)
        slope[...] = grade
        total[...] = jnp.zeros_like(total)

    part = jnp.concatenate([p0[...], p1[...], p2[...], p3[...], p4[...]], axis=0)
    total[...] += jnp.dot(part, w_down[...], preferred_element_type=F32)

    @pl.when(step == STEPS - 1)
    def _():
        d_act = (total[...] * slope[...]).astype(BF16)
        back = lax.dot_general(
            d_act, tied[...], (((1,), (1,)), ((), ())), preferred_element_type=F32
        ).astype(BF16)
        for k in range(16):
            codes_part[block(k)] = back[k * count : (k + 1) * count, :]
        outer = lax.dot_general(
            rows[...], d_act, (((0,), (0,)), ((), ())), preferred_element_type=F32
        ).astype(BF16)
        piece = outer.shape[0] // 8
        for k in range(8):
            to_core = (k // 4 + core) % 2
            inner[to_core, (k % 4 + 4 - x) % 4] = outer[k * piece : (k + 1) * piece, :]


def hidden_call(at, codes, tied, w_down, pieces):
    features, units = w_down.shape
    tokens = sum(p.shape[0] for p in pieces)
    width = tied.shape[0]
    span = features // STEPS
    whole = lambda shape: pl.BlockSpec(shape, lambda i, at: (0,) * len(shape))
    out = [
        jax.ShapeDtypeStruct((tokens, units), BF16),
        jax.ShapeDtypeStruct(codes.shape, BF16),
        jax.ShapeDtypeStruct((2, 4, width // 8, units), BF16),
    ]
    return pl.pallas_call(
        hidden_kernel,
        grid_spec=pltpu.PrefetchScalarGridSpec(
            num_scalar_prefetch=1,
            grid=(STEPS,),
            in_specs=[
                whole(codes.shape),
                whole(tied.shape),
                pl.BlockSpec((span, units), lambda i, at: (i, 0)),
            ]
            + [pl.BlockSpec((p.shape[0], span), lambda i, at: (0, i)) for p in pieces],
            out_specs=[whole(o.shape) for o in out],
            scratch_shapes=[
                pltpu.VMEM((tokens, width), BF16),
                pltpu.VMEM((tokens, units), F32),
                pltpu.VMEM((tokens, units), F32),
            ],
        ),
        out_shape=out,
        compiler_params=pltpu.CompilerParams(vmem_limit_bytes=VMEM),
        cost_estimate=pl.CostEstimate(
            flops=2 * tokens * units * (features + 3 * width),
            bytes_accessed=2 * (features * units + tokens * features),
            transcendentals=2 * tokens * units,
        ),
    )(at, codes, tied, w_down, *pieces)


def term_kernel(at, hidden, p0, p1, p2, p3, p4, keep, give):
    part = jnp.concatenate([p0[...], p1[...], p2[...], p3[...], p4[...]], axis=0)
    term = lax.dot_general(
        part, hidden[...], (((0,), (0,)), ((), ())), preferred_element_type=F32
    ).astype(BF16)
    half = term.shape[0] // 2
    first, second = term[:half], term[half:]

    @pl.when(at[2] == 0)
    def _():
        keep[0, 0] = first
        give[0, 0] = second

    @pl.when(at[2] != 0)
    def _():
        keep[0, 0] = second
        give[0, 0] = first


def term_call(at, hidden, pieces):
    tokens, units = hidden.shape
    features = pieces[0].shape[1]
    span = features // 8

    def place(i, at):
        return ((i % 4 + 4 - at[3]) % 4, (i // 4 + at[4]) % 2, 0, 0)

    out = [jax.ShapeDtypeStruct((4, 2, span // 2, units), BF16)] * 2
    return pl.pallas_call(
        term_kernel,
        grid_spec=pltpu.PrefetchScalarGridSpec(
            num_scalar_prefetch=1,
            grid=(8,),
            in_specs=[pl.BlockSpec((tokens, units), lambda i, at: (0, 0))]
            + [pl.BlockSpec((p.shape[0], span), lambda i, at: (0, i)) for p in pieces],
            out_specs=[pl.BlockSpec((1, 1, span // 2, units), place)] * 2,
        ),
        out_shape=out,
        compiler_params=pltpu.CompilerParams(vmem_limit_bytes=VMEM),
        cost_estimate=pl.CostEstimate(
            flops=2 * tokens * units * features,
            bytes_accessed=2 * (features * units + tokens * features),
            transcendentals=0,
        ),
    )(at, hidden, *pieces)


def on_device(tokens, gain, encoder, w_up, w_down, cotangent):
    rows, width = encoder.shape
    own = rows // 16
    dp_at = lax.axis_index("dp")
    mp_at = lax.axis_index("mp")
    core, x, far = dp_at % 2, (dp_at // 2) % 4, dp_at // 8

    z, y = mp_at // 4, mp_at % 4
    tie = lax.optimization_barrier

    other = send(encoder, "dp", step_far)
    as_float = tokens.astype(F32)
    center = as_float - jnp.mean(as_float, axis=1, keepdims=True)
    inv_std = lax.rsqrt(jnp.mean(center * center, axis=1, keepdims=True) + 1e-06)
    unit = center * inv_std
    normed = (unit * gain).astype(BF16)
    other, normed, late_cotangent = tie((other, normed, cotangent))
    parts = gather_parts(jnp.stack(pair_in_order(encoder, other, far)), "dp", step_x)
    line = gather_parts(late_cotangent, "mp", step_z)
    *parts, line = tie((*parts, jnp.concatenate(line)))
    along = in_order(parts, x)
    across = send(along, "dp", step_core)
    after = send(line, "mp", step_y(-1))
    before = send(line, "mp", step_y(1))
    full_encoder = join_encoder(along, across, core)
    code_rows = jnp.dot(normed, full_encoder, preferred_element_type=F32).astype(BF16)
    all_codes = gather_codes(code_rows)
    after, before, _ = tie((after, before, code_rows))
    half = line.shape[0] // 2
    far_a = send(after[:half], "mp", step_y(-1))
    far_b = send(before[half:], "mp", step_y(1))
    tied_up = jnp.einsum("dc,df->cf", full_encoder, w_up, preferred_element_type=F32).astype(BF16)
    all_codes, late_normed = tie((all_codes, normed))
    normed_cols = lax.all_to_all(late_normed, "dp", split_axis=1, concat_axis=0, tiled=True)
    all_codes, tied_up, normed_cols, far_a, far_b = tie(
        (all_codes, tied_up, normed_cols, far_a, far_b)
    )
    at = jnp.stack([z, y, core, x, far]).astype(jnp.int32)
    pieces = (line, after, far_a, far_b, before)
    hidden, codes_part, inner = hidden_call(at, all_codes, tied_up, w_down, pieces)
    grad_codes = scatter_codes(codes_part).astype(BF16)
    keep, give = term_call(at, hidden, pieces)
    term = add(keep, send(give, "dp", step_core)).astype(BF16)
    inner = add(inner[0], send(inner[1], "dp", step_core)).astype(BF16)
    term, inner = tie((term, inner))
    got_a = send(term[2, 0], "dp", step_x(1))
    got_b = send(term[2, 1], "dp", step_x(-1))
    got = [send(inner[k], "dp", step_x(k)) for k in (1, 2, 3)]
    inner = (inner[0].astype(F32) + sum(g.astype(F32) for g in got)).astype(BF16)
    got_a, got_b, inner, grad_codes = tie((got_a, got_b, inner, grad_codes))
    up = jnp.stack([add(term[1, 0], got_a).astype(BF16), term[1, 1]])
    down = jnp.stack([term[3, 0], add(term[3, 1], got_b).astype(BF16)])
    count, cols = inner.shape
    mine = jnp.concatenate([inner, grad_codes.reshape(-1, cols)])
    up, down, mine = tie((up, down, mine))
    other = send(mine, "dp", step_far)
    up = send(up, "dp", step_x(1))
    down = send(down, "dp", step_x(-1))
    inner = add(inner, other[:count]).astype(BF16)
    mine = jnp.concatenate([inner, *pair_in_order(mine[count:], other[count:], far)])
    parts = gather_parts(mine, "dp", step_x)
    up, down, *parts = tie((up, down, *parts))
    total = [term[0, k].astype(F32) + up[k].astype(F32) + down[k].astype(F32) for k in (0, 1)]
    grad_down = total[0] + send(total[1].astype(BF16), "dp", step_far).astype(F32)
    mine = in_order(parts, x)
    both = jnp.stack(pair_in_order(mine, send(mine, "dp", step_core), core))
    inner = both[:, :, :count].reshape(-1, cols)
    codes_cols = both[:, :, count:].reshape(-1, width)
    up_rows = lax.dynamic_slice_in_dim(w_up, dp_at * rows, rows, 0)
    decode_part = jnp.einsum("df,cf->dc", up_rows, inner, preferred_element_type=F32)
    count = tokens.shape[0]
    normed_cols = normed_cols.reshape(2, 4, 2, count, rows).transpose(2, 1, 0, 3, 4)
    normed_cols = normed_cols.reshape(16 * count, rows)
    encode_part = jnp.einsum("td,tc->dc", normed_cols, codes_cols, preferred_element_type=F32)
    both = jnp.concatenate([encode_part, decode_part], axis=1).astype(BF16)
    both = lax.all_to_all(both.reshape(16, own, 2 * width), "mp", split_axis=0, concat_axis=0)
    both = jnp.sum(both.astype(F32), axis=0)
    grad_up = jnp.dot(encoder, inner, preferred_element_type=F32)
    own_encoder = lax.dynamic_slice_in_dim(encoder, mp_at * own, own, 0).astype(F32)
    own_gain = lax.dynamic_slice_in_dim(gain, dp_at * rows + mp_at * own, own, 0)
    grad_encoder = both[:, :width] + both[:, width:]
    grad_gain = jnp.sum(own_encoder * both[:, :width], axis=1) / own_gain
    d_normed = jnp.einsum("tc,dc->td", grad_codes, full_encoder, preferred_element_type=F32)
    dx_hat = d_normed * gain
    mean_one = jnp.mean(dx_hat, axis=1, keepdims=True)
    mean_two = jnp.mean(dx_hat * unit, axis=1, keepdims=True)
    grad_tokens = (
        cotangent.astype(F32) + inv_std * (dx_hat - mean_one - unit * mean_two)
    ).astype(BF16)
    return (grad_tokens, grad_up, grad_down, grad_encoder, grad_gain)


def solution(mesh):
    placed = (
        P(("dp", "mp"), None),
        P(),
        P("dp", None),
        P(None, "mp"),
        P(None, "mp"),
        P(("dp", "mp"), None),
    )
    return jax.shard_map(
        on_device,
        mesh=mesh,
        in_specs=placed,
        out_specs=(
            P(("dp", "mp"), None),
            P("dp", "mp"),
            P("dp", "mp"),
            P(("dp", "mp"), None),
            P(("dp", "mp")),
        ),
        check_vma=False,
    )
```

```python
import jax
import jax.numpy as jnp
from jax import lax
from jax.experimental import pallas as pl
from jax.experimental.pallas import tpu as pltpu
from jax.sharding import PartitionSpec as P

F32 = jnp.float32
BF16 = jnp.bfloat16


def step_core(i):
    return i ^ 1


def step_far(i):
    return i ^ 8


def step_x(k):
    return lambda i: (i & 9) | ((((i >> 1) + k) & 3) << 1)


def step_y(k):
    return lambda i: (i & 12) | ((i + k) & 3)


def step_z(k):
    return lambda i: ((((i >> 2) + k) & 3) << 2) | (i & 3)


def send(value, axis, target):
    return lax.ppermute(value, axis, [(i, target(i)) for i in range(16)])


def gather_parts(value, axis, step):
    return [value] + [send(value, axis, step(-k)) for k in (1, 2, 3)]


def in_order(parts, at):
    n = len(parts)
    twice = jnp.stack(parts + parts[:-1])
    return lax.dynamic_slice_in_dim(twice, (n - at) % n, n, 0)


def pair_in_order(mine, other, at):
    first = jnp.where(at == 0, mine, other)
    second = jnp.where(at == 0, other, mine)
    return first, second


def pick(value, at, axis):
    return lax.dynamic_index_in_dim(value, at, axis, keepdims=False)


def gelu_parts(pre_act):
    cdf_part = 0.5 * (1.0 + lax.erf(pre_act * 0.7071067811865476))
    density = jnp.exp(-0.5 * pre_act * pre_act) * 0.3989422804014327
    return (pre_act * cdf_part, cdf_part + pre_act * density)


def add(a, b):
    return a.astype(F32) + b.astype(F32)


def join_encoder(along, across, core):
    width = along.shape[1]
    full = jnp.stack(pair_in_order(along, across, core)).reshape(2, 4, 2, -1, width)
    return full.transpose(2, 1, 0, 3, 4).reshape(-1, width)


def gather_codes(code_rows):
    count, width = code_rows.shape
    return lax.all_to_all(
        jnp.broadcast_to(code_rows, (16, count, width)), "mp", split_axis=0, concat_axis=0
    )


def scatter_codes(part):
    got = lax.all_to_all(part, "mp", split_axis=0, concat_axis=0)
    return jnp.sum(got.astype(F32), axis=0)


VMEM = 58 * 1024 * 1024
SMALL = 16 * 1024 * 1024


def token_block(k, at):
    return ((at[0] + k % 4) % 4) * 4 + (at[1] + k // 4) % 4


def fill_rows(at, codes, rows):
    count = codes.shape[1]
    for k in range(16):
        rows[k * count : (k + 1) * count, :] = codes[token_block(k, at)]


def row_copies(pieces, rows, sems):
    copies, start = [], 0
    for k, piece in enumerate(pieces):
        count = piece.shape[0]
        copies.append(
            pltpu.make_async_copy(piece, rows.at[pl.ds(start, count), :], sems.at[k])
        )
        start += count
    return copies


def whole(shape):
    return pl.BlockSpec(shape, lambda i, at: (0,) * len(shape))


def mlp_kernel(at, codes, tied, w_down, *refs):
    pieces, (keep, give, codes_part, inner) = refs[:5], refs[5:9]
    rows, hidden, slope, total, upstream, weights, sems = refs[9:]
    step = pl.program_id(0)
    span = 2 * keep.shape[2]
    here = pl.ds(pl.multiple_of(step * span, span), span)

    def weight_copy(k):
        part = pl.ds(pl.multiple_of(k * span, span), span)
        return pltpu.make_async_copy(w_down.at[part, :], weights.at[part, :], sems.at[5 + k])

    @pl.when(step == 0)
    def _():
        copies = row_copies(pieces, upstream, sems)
        for c in copies:
            c.start()
        for k in range(8):
            weight_copy(k).start()
        fill_rows(at, codes, rows)
        pre_act = jnp.dot(rows[...], tied[...], preferred_element_type=F32)
        value, grade = gelu_parts(pre_act)
        hidden[...] = value.astype(BF16)
        slope[...] = grade
        total[...] = jnp.zeros_like(total)
        for c in copies:
            c.wait()

    weight_copy(step).wait()
    part = upstream[:, here]
    total[...] += jnp.dot(part, weights[here, :], preferred_element_type=F32)
    term = lax.dot_general(
        part, hidden[...], (((0,), (0,)), ((), ())), preferred_element_type=F32
    ).astype(BF16)
    half = term.shape[0] // 2
    first, second = term[:half], term[half:]

    @pl.when(at[2] == 0)
    def _():
        keep[0, 0] = first
        give[0, 0] = second

    @pl.when(at[2] != 0)
    def _():
        keep[0, 0] = second
        give[0, 0] = first

    @pl.when(step == 7)
    def _():
        d_act = (total[...] * slope[...]).astype(BF16)
        back = lax.dot_general(
            d_act, tied[...], (((1,), (1,)), ((), ())), preferred_element_type=F32
        ).astype(BF16)
        count = codes.shape[1]
        for k in range(16):
            codes_part[token_block(k, at)] = back[k * count : (k + 1) * count, :]
        outer = lax.dot_general(
            rows[...], d_act, (((0,), (0,)), ((), ())), preferred_element_type=F32
        ).astype(BF16)
        piece = outer.shape[0] // 8
        for k in range(8):
            to_core = (k // 4 + at[2]) % 2
            inner[to_core, (k % 4 + 4 - at[3]) % 4] = outer[k * piece : (k + 1) * piece, :]


def mlp_call(at, codes, tied, w_down, pieces):
    width, units = tied.shape
    tokens = codes.shape[0] * codes.shape[1]
    features = w_down.shape[0]
    span = features // 8

    def place(i, at):
        return ((i % 4 + 4 - at[3]) % 4, (i // 4 + at[4]) % 2, 0, 0)

    out = [jax.ShapeDtypeStruct((4, 2, span // 2, units), BF16)] * 2
    out += [
        jax.ShapeDtypeStruct(codes.shape, BF16),
        jax.ShapeDtypeStruct((2, 4, width // 8, units), BF16),
    ]
    return pl.pallas_call(
        mlp_kernel,
        grid_spec=pltpu.PrefetchScalarGridSpec(
            num_scalar_prefetch=1,
            grid=(8,),
            in_specs=[whole(codes.shape), whole(tied.shape)]
            + [pl.BlockSpec(memory_space=pltpu.HBM)]
            + [pl.BlockSpec(memory_space=pltpu.HBM)] * 5,
            out_specs=[pl.BlockSpec((1, 1, span // 2, units), place)] * 2
            + [whole(o.shape) for o in out[2:]],
            scratch_shapes=[
                pltpu.VMEM((tokens, width), BF16),
                pltpu.VMEM((tokens, units), BF16),
                pltpu.VMEM((tokens, units), F32),
                pltpu.VMEM((tokens, units), F32),
                pltpu.VMEM((tokens, features), BF16),
                pltpu.VMEM((features, units), BF16),
                pltpu.SemaphoreType.DMA((13,)),
            ],
        ),
        out_shape=out,
        compiler_params=pltpu.CompilerParams(vmem_limit_bytes=VMEM),
        cost_estimate=pl.CostEstimate(
            flops=4 * tokens * units * (features + width),
            bytes_accessed=2 * (3 * features * units + tokens * features),
            transcendentals=2 * tokens * units,
        ),
    )(at, codes, tied, w_down, *pieces)


def tied_kernel(at, along, across, w_up, out, total):
    step = pl.program_id(0)
    mine, other = along[0], across[0]
    lower = at[2] == 0
    block = jnp.concatenate(
        [jnp.where(lower, mine, other), jnp.where(lower, other, mine)], axis=0
    )
    part = lax.dot_general(
        block, w_up[...], (((0,), (0,)), ((), ())), preferred_element_type=F32
    )

    @pl.when(step == 0)
    def _():
        total[...] = part

    @pl.when(step != 0)
    def _():
        total[...] += part

    @pl.when(step == 7)
    def _():
        out[...] = total[...].astype(BF16)


def tied_call(at, along, across, w_up):
    rows, width = along.shape[0] // 8, along.shape[1]
    units = w_up.shape[1]
    block = pl.BlockSpec((1, rows, width), lambda i, at: (i, 0, 0))
    return pl.pallas_call(
        tied_kernel,
        grid_spec=pltpu.PrefetchScalarGridSpec(
            num_scalar_prefetch=1,
            grid=(8,),
            in_specs=[
                block,
                block,
                pl.BlockSpec((2 * rows, units), lambda i, at: (i % 2 * 4 + i // 2, 0)),
            ],
            out_specs=whole((width, units)),
            scratch_shapes=[pltpu.VMEM((width, units), F32)],
        ),
        out_shape=jax.ShapeDtypeStruct((width, units), BF16),
        compiler_params=pltpu.CompilerParams(vmem_limit_bytes=SMALL),
        cost_estimate=pl.CostEstimate(
            flops=32 * rows * width * units, bytes_accessed=64 * rows * units, transcendentals=0
        ),
    )(at, along.reshape(8, rows, width), across.reshape(8, rows, width), w_up)


def rows_kernel(at, normed, w_up, encoder, *refs):
    parts, (both, grad_up, inner, codes, sums) = (refs[:4], refs[4:8]), refs[8:]
    width = encoder.shape[1]
    units = w_up.shape[1]
    count = inner.shape[0] // 8
    for c in range(2):
        for k in range(4):
            part = parts[c][k]
            place = ((at[2] + c) % 2 * 4 + (at[3] + k) % 4) * count
            inner[pl.ds(pl.multiple_of(place, count), count), :] = part[:count, :]
            place = (c * 4 + (4 - k) % 4) * 64
            for j in range(4):
                codes[place + 16 * j : place + 16 * (j + 1), :] = part[
                    count + 16 * (j // 2) : count + 16 * (j // 2 + 1),
                    width * (j % 2) : width * (j % 2 + 1),
                ]
    sums[:, :width] = lax.dot_general(
        normed[...], codes[...], (((0,), (0,)), ((), ())), preferred_element_type=F32
    )
    sums[:, width:] = lax.dot_general(
        w_up[...], inner[...], (((1,), (1,)), ((), ())), preferred_element_type=F32
    )
    own = both.shape[1]
    for k in range(16):
        both[k] = sums[k * own : (k + 1) * own, :].astype(BF16)
    grad_up[...] = jnp.dot(encoder[...], inner[...], preferred_element_type=F32)


def rows_call(at, normed, w_up, encoder, parts, others):
    tokens, rows = normed.shape
    width, units = encoder.shape[1], w_up.shape[1]
    out = [
        jax.ShapeDtypeStruct((16, rows // 16, 2 * width), BF16),
        jax.ShapeDtypeStruct((rows, units), F32),
    ]
    return pl.pallas_call(
        rows_kernel,
        grid_spec=pltpu.PrefetchScalarGridSpec(
            num_scalar_prefetch=1,
            grid=(1,),
            in_specs=[
                whole(normed.shape),
                pl.BlockSpec((rows, units), lambda i, at: (at[5], 0)),
                whole(encoder.shape),
            ]
            + [whole(parts[0].shape)] * 8,
            out_specs=[whole(o.shape) for o in out],
            scratch_shapes=[
                pltpu.VMEM((width, units), BF16),
                pltpu.VMEM((tokens, width), BF16),
                pltpu.VMEM((rows, 2 * width), F32),
            ],
        ),
        out_shape=out,
        compiler_params=pltpu.CompilerParams(vmem_limit_bytes=SMALL),
        cost_estimate=pl.CostEstimate(
            flops=2 * rows * width * (tokens + 2 * units),
            bytes_accessed=2 * rows * (tokens + 3 * units),
            transcendentals=0,
        ),
    )(at, normed, w_up, encoder, *parts, *others)


def on_device(tokens, gain, encoder, w_up, w_down, cotangent):
    rows, width = encoder.shape
    own = rows // 16
    dp_at = lax.axis_index("dp")
    mp_at = lax.axis_index("mp")
    core, x, far = dp_at % 2, (dp_at // 2) % 4, dp_at // 8

    z, y = mp_at // 4, mp_at % 4
    tie = lax.optimization_barrier

    other = send(encoder, "dp", step_far)
    as_float = tokens.astype(F32)
    center = as_float - jnp.mean(as_float, axis=1, keepdims=True)
    inv_std = lax.rsqrt(jnp.mean(center * center, axis=1, keepdims=True) + 1e-06)
    unit = center * inv_std
    normed = (unit * gain).astype(BF16)
    spread = normed.reshape(-1, 2, 4, 2, rows).transpose(3, 0, 2, 1, 4).reshape(2, -1, 8 * rows)
    mine, theirs = pick(spread, core, 0), pick(spread, 1 - core, 0)
    other, normed, late_cotangent = tie((other, normed, cotangent))
    parts = gather_parts(jnp.stack(pair_in_order(encoder, other, far)), "dp", step_x)
    line = gather_parts(late_cotangent, "mp", step_z)
    blocks = normed.reshape(-1, 2, 4, 2, rows).transpose(3, 2, 1, 0, 4)
    got = send(pick(blocks, 1 - core, 0), "dp", step_core)
    along = in_order(parts, x).reshape(8 * rows, width)
    along, line, got = tie((along, jnp.concatenate(line), got))
    across = send(along, "dp", step_core)
    after = send(line, "mp", step_y(-1))
    before = send(line, "mp", step_y(1))
    code_rows = jnp.dot(mine, along, preferred_element_type=F32)
    code_rows += jnp.dot(theirs, across, preferred_element_type=F32)
    code_rows = code_rows.astype(BF16)
    all_codes = gather_codes(code_rows)
    blocks = jnp.stack([pick(blocks, core, 0), got], axis=2)
    got = [send(pick(blocks, (x + k) % 4, 0), "dp", step_x(k)) for k in (1, 2, 3)]
    after, before, _, *got = tie((after, before, code_rows, *got))
    blocks = jnp.stack([pick(blocks, x, 0), *got], axis=2)
    half = line.shape[0] // 2
    far_a = send(after[:half], "mp", step_y(-1))
    far_b = send(before[half:], "mp", step_y(1))
    got = send(pick(blocks, 1 - far, 0), "dp", step_far)
    at = jnp.stack([z, y, core, x, far, dp_at]).astype(jnp.int32)
    tied_up = tied_call(at, along, across, w_up)
    all_codes, tied_up, far_a, far_b, got = tie((all_codes, tied_up, far_a, far_b, got))
    normed_cols = jnp.stack([pick(blocks, far, 0), got], axis=2).reshape(-1, rows)
    pieces = (line, after, far_a, far_b, before)
    keep, give, codes_part, inner = mlp_call(at, all_codes, tied_up, w_down, pieces)
    sent = send(give, "dp", step_core)
    grad_codes = scatter_codes(codes_part).astype(BF16)
    inner = add(inner[0], send(inner[1], "dp", step_core)).astype(BF16)
    first, second = [add(keep[2, k], sent[2, k]).astype(BF16) for k in (0, 1)]
    first, second, inner = tie((first, second, inner))
    got_a = send(first, "dp", step_x(1))
    got_b = send(second, "dp", step_x(-1))
    got = [send(inner[k], "dp", step_x(k)) for k in (1, 2, 3)]
    inner = (inner[0].astype(F32) + sum(g.astype(F32) for g in got)).astype(BF16)
    got_a, got_b, inner, grad_codes = tie((got_a, got_b, inner, grad_codes))
    up = [add(keep[1, 0], sent[1, 0]) + got_a.astype(F32), add(keep[1, 1], sent[1, 1])]
    down = [add(keep[3, 0], sent[3, 0]), add(keep[3, 1], sent[3, 1]) + got_b.astype(F32)]
    up = jnp.stack([u.astype(BF16) for u in up])
    down = jnp.stack([d.astype(BF16) for d in down])
    count, cols = inner.shape
    halves = jnp.split(grad_codes, 2)
    mine = jnp.concatenate([inner, jnp.concatenate(halves, axis=1)])
    up, down, mine = tie((up, down, mine))
    other = send(mine, "dp", step_far)
    up = send(up, "dp", step_x(1))
    down = send(down, "dp", step_x(-1))
    inner = add(inner, other[:count]).astype(BF16)
    mine = jnp.concatenate([inner, mine[count:], other[count:]])
    parts = gather_parts(mine, "dp", step_x)
    up, down, *parts = tie((up, down, *parts))
    total = [add(keep[0, k], sent[0, k]) + add(up[k], down[k]) for k in (0, 1)]
    grad_down = total[0] + send(total[1].astype(BF16), "dp", step_far).astype(F32)
    others = [send(p, "dp", step_core) for p in parts]
    both, grad_up = rows_call(at, normed_cols, w_up, encoder, parts, others)
    both = lax.all_to_all(both, "mp", split_axis=0, concat_axis=0)
    both = jnp.sum(both.astype(F32), axis=0)
    own_encoder = lax.dynamic_slice_in_dim(encoder, mp_at * own, own, 0).astype(F32)
    own_gain = lax.dynamic_slice_in_dim(gain, dp_at * rows + mp_at * own, own, 0)
    grad_encoder = both[:, :width] + both[:, width:]
    grad_gain = jnp.sum(own_encoder * both[:, :width], axis=1) / own_gain
    full_encoder = join_encoder(along, across, core)
    d_normed = jnp.einsum("tc,dc->td", grad_codes, full_encoder, preferred_element_type=F32)
    dx_hat = d_normed * gain
    mean_one = jnp.mean(dx_hat, axis=1, keepdims=True)
    mean_two = jnp.mean(dx_hat * unit, axis=1, keepdims=True)
    grad_tokens = (
        cotangent.astype(F32) + inv_std * (dx_hat - mean_one - unit * mean_two)
    ).astype(BF16)
    return (grad_tokens, grad_up, grad_down, grad_encoder, grad_gain)


def solution(mesh):
    placed = (
        P(("dp", "mp"), None),
        P(),
        P("dp", None),
        P(None, "mp"),
        P(None, "mp"),
        P(("dp", "mp"), None),
    )
    return jax.shard_map(
        on_device,
        mesh=mesh,
        in_specs=placed,
        out_specs=(
            P(("dp", "mp"), None),
            P("dp", "mp"),
            P("dp", "mp"),
            P(("dp", "mp"), None),
            P(("dp", "mp")),
        ),
        check_vma=False,
    )
```

```python
import jax
import jax.numpy as jnp
from jax import lax
from jax.experimental import pallas as pl
from jax.experimental.pallas import tpu as pltpu
from jax.sharding import PartitionSpec as P

F32 = jnp.float32
BF16 = jnp.bfloat16


def step_core(i):
    return i ^ 1


def step_far(i):
    return i ^ 8


def step_x(k):
    return lambda i: (i & 9) | ((((i >> 1) + k) & 3) << 1)


def step_y(k):
    return lambda i: (i & 12) | ((i + k) & 3)


def step_z(k):
    return lambda i: ((((i >> 2) + k) & 3) << 2) | (i & 3)


def send(value, axis, target):
    return lax.ppermute(value, axis, [(i, target(i)) for i in range(16)])


def gather_parts(value, axis, step):
    return [value] + [send(value, axis, step(-k)) for k in (1, 2, 3)]


def in_order(parts, at):
    n = len(parts)
    twice = jnp.stack(parts + parts[:-1])
    return lax.dynamic_slice_in_dim(twice, (n - at) % n, n, 0)


def pair_in_order(mine, other, at):
    first = jnp.where(at == 0, mine, other)
    second = jnp.where(at == 0, other, mine)
    return first, second


def pick(value, at, axis):
    return lax.dynamic_index_in_dim(value, at, axis, keepdims=False)


def gelu_parts(pre_act):
    cdf_part = 0.5 * (1.0 + lax.erf(pre_act * 0.7071067811865476))
    density = jnp.exp(-0.5 * pre_act * pre_act) * 0.3989422804014327
    return (pre_act * cdf_part, cdf_part + pre_act * density)


def add(a, b):
    return a.astype(F32) + b.astype(F32)


def join_encoder(along, across, core):
    width = along.shape[1]
    full = jnp.stack(pair_in_order(along, across, core)).reshape(2, 4, 2, -1, width)
    return full.transpose(2, 1, 0, 3, 4).reshape(-1, width)


def gather_codes(code_rows):
    count, width = code_rows.shape
    return lax.all_to_all(
        jnp.broadcast_to(code_rows, (16, count, width)), "mp", split_axis=0, concat_axis=0
    )


def scatter_codes(part):
    got = lax.all_to_all(part, "mp", split_axis=0, concat_axis=0)
    return jnp.sum(got.astype(F32), axis=0)


VMEM = 58 * 1024 * 1024
SMALL = 16 * 1024 * 1024


def token_block(k, at):
    return ((at[0] + k % 4) % 4) * 4 + (at[1] + k // 4) % 4


def fill_rows(at, codes, rows):
    count = codes.shape[1]
    for k in range(16):
        rows[k * count : (k + 1) * count, :] = codes[token_block(k, at)]


def row_copies(pieces, rows, sems):
    copies, start = [], 0
    for k, piece in enumerate(pieces):
        count = piece.shape[0]
        copies.append(
            pltpu.make_async_copy(piece, rows.at[pl.ds(start, count), :], sems.at[k])
        )
        start += count
    return copies


def whole(shape):
    return pl.BlockSpec(shape, lambda i, at: (0,) * len(shape))


def mlp_kernel(at, codes, tied, w_down, *refs):
    pieces, (keep, give, codes_part, inner, inner_give) = refs[:5], refs[5:10]
    rows, hidden, slope, total, upstream, weights, sems = refs[10:]
    step = pl.program_id(0)
    span = 2 * keep.shape[2]
    here = pl.ds(pl.multiple_of(step * span, span), span)

    def weight_copy(k):
        part = pl.ds(pl.multiple_of(k * span, span), span)
        return pltpu.make_async_copy(w_down.at[part, :], weights.at[part, :], sems.at[5 + k])

    @pl.when(step == 0)
    def _():
        copies = row_copies(pieces, upstream, sems)
        for c in copies:
            c.start()
        for k in range(8):
            weight_copy(k).start()
        fill_rows(at, codes, rows)
        pre_act = jnp.dot(rows[...], tied[...], preferred_element_type=F32)
        value, grade = gelu_parts(pre_act)
        hidden[...] = value.astype(BF16)
        slope[...] = grade
        total[...] = jnp.zeros_like(total)
        for c in copies:
            c.wait()

    weight_copy(step).wait()
    part = upstream[:, here]
    total[...] += jnp.dot(part, weights[here, :], preferred_element_type=F32)
    term = lax.dot_general(
        part, hidden[...], (((0,), (0,)), ((), ())), preferred_element_type=F32
    ).astype(BF16)
    half = term.shape[0] // 2
    first, second = term[:half], term[half:]

    @pl.when(at[2] == 0)
    def _():
        keep[0, 0] = first
        give[0, 0] = second

    @pl.when(at[2] != 0)
    def _():
        keep[0, 0] = second
        give[0, 0] = first

    @pl.when(step == 7)
    def _():
        d_act = (total[...] * slope[...]).astype(BF16)
        back = lax.dot_general(
            d_act, tied[...], (((1,), (1,)), ((), ())), preferred_element_type=F32
        ).astype(BF16)
        count = codes.shape[1]
        for k in range(16):
            codes_part[token_block(k, at)] = back[k * count : (k + 1) * count, :]
        outer = lax.dot_general(
            rows[...], d_act, (((0,), (0,)), ((), ())), preferred_element_type=F32
        ).astype(BF16)
        piece = outer.shape[0] // 8
        lower = at[2] == 0
        for k in range(4):
            first = outer[k * piece : (k + 1) * piece, :]
            second = outer[(k + 4) * piece : (k + 5) * piece, :]
            inner[(k + 4 - at[3]) % 4] = jnp.where(lower, first, second)
            inner_give[(k + 4 - at[3]) % 4] = jnp.where(lower, second, first)


def mlp_call(at, codes, tied, w_down, pieces):
    width, units = tied.shape
    tokens = codes.shape[0] * codes.shape[1]
    features = w_down.shape[0]
    span = features // 8

    def place(i, at):
        return ((i % 4 + 4 - at[3]) % 4, (i // 4 + at[4]) % 2, 0, 0)

    out = [jax.ShapeDtypeStruct((4, 2, span // 2, units), BF16)] * 2
    out += [
        jax.ShapeDtypeStruct(codes.shape, BF16),
        jax.ShapeDtypeStruct((4, width // 8, units), BF16),
        jax.ShapeDtypeStruct((4, width // 8, units), BF16),
    ]
    return pl.pallas_call(
        mlp_kernel,
        grid_spec=pltpu.PrefetchScalarGridSpec(
            num_scalar_prefetch=1,
            grid=(8,),
            in_specs=[whole(codes.shape), whole(tied.shape)]
            + [pl.BlockSpec(memory_space=pltpu.HBM)]
            + [pl.BlockSpec(memory_space=pltpu.HBM)] * 5,
            out_specs=[pl.BlockSpec((1, 1, span // 2, units), place)] * 2
            + [whole(o.shape) for o in out[2:]],
            scratch_shapes=[
                pltpu.VMEM((tokens, width), BF16),
                pltpu.VMEM((tokens, units), BF16),
                pltpu.VMEM((tokens, units), F32),
                pltpu.VMEM((tokens, units), F32),
                pltpu.VMEM((tokens, features), BF16),
                pltpu.VMEM((features, units), BF16),
                pltpu.SemaphoreType.DMA((13,)),
            ],
        ),
        out_shape=out,
        compiler_params=pltpu.CompilerParams(vmem_limit_bytes=VMEM),
        cost_estimate=pl.CostEstimate(
            flops=4 * tokens * units * (features + width),
            bytes_accessed=2 * (3 * features * units + tokens * features),
            transcendentals=2 * tokens * units,
        ),
    )(at, codes, tied, w_down, *pieces)


def tied_kernel(at, along, across, w_up, out, total):
    step = pl.program_id(0)
    mine, other = along[0], across[0]
    lower = at[2] == 0
    block = jnp.concatenate(
        [jnp.where(lower, mine, other), jnp.where(lower, other, mine)], axis=0
    )
    part = lax.dot_general(
        block, w_up[...], (((0,), (0,)), ((), ())), preferred_element_type=F32
    )

    @pl.when(step == 0)
    def _():
        total[...] = part

    @pl.when(step != 0)
    def _():
        total[...] += part

    @pl.when(step == 7)
    def _():
        out[...] = total[...].astype(BF16)


def tied_call(at, along, across, w_up):
    rows, width = along.shape[0] // 8, along.shape[1]
    units = w_up.shape[1]
    block = pl.BlockSpec((1, rows, width), lambda i, at: (i, 0, 0))
    return pl.pallas_call(
        tied_kernel,
        grid_spec=pltpu.PrefetchScalarGridSpec(
            num_scalar_prefetch=1,
            grid=(8,),
            in_specs=[
                block,
                block,
                pl.BlockSpec((2 * rows, units), lambda i, at: (i % 2 * 4 + i // 2, 0)),
            ],
            out_specs=whole((width, units)),
            scratch_shapes=[pltpu.VMEM((width, units), F32)],
        ),
        out_shape=jax.ShapeDtypeStruct((width, units), BF16),
        compiler_params=pltpu.CompilerParams(vmem_limit_bytes=SMALL),
        cost_estimate=pl.CostEstimate(
            flops=32 * rows * width * units, bytes_accessed=64 * rows * units, transcendentals=0
        ),
    )(at, along.reshape(8, rows, width), across.reshape(8, rows, width), w_up)


def rows_kernel(at, normed, w_up, encoder, *refs):
    parts, (both, grad_up, inner, codes, sums) = (refs[:4], refs[4:8]), refs[8:]
    width = encoder.shape[1]
    units = w_up.shape[1]
    count = inner.shape[0] // 8
    for c in range(2):
        for k in range(4):
            part = parts[c][k]
            place = ((at[2] + c) % 2 * 4 + (at[3] + k) % 4) * count
            inner[pl.ds(pl.multiple_of(place, count), count), :] = part[:count, :]
            place = (c * 4 + (4 - k) % 4) * 64
            for j in range(4):
                codes[place + 16 * j : place + 16 * (j + 1), :] = part[
                    count + 16 * (j // 2) : count + 16 * (j // 2 + 1),
                    width * (j % 2) : width * (j % 2 + 1),
                ]
    sums[:, :width] = lax.dot_general(
        normed[...], codes[...], (((0,), (0,)), ((), ())), preferred_element_type=F32
    )
    sums[:, width:] = lax.dot_general(
        w_up[...], inner[...], (((1,), (1,)), ((), ())), preferred_element_type=F32
    )
    own = both.shape[1]
    for k in range(16):
        both[k] = sums[k * own : (k + 1) * own, :].astype(BF16)
    grad_up[...] = jnp.dot(encoder[...], inner[...], preferred_element_type=F32)


def rows_call(at, normed, w_up, encoder, parts, others):
    tokens, rows = normed.shape
    width, units = encoder.shape[1], w_up.shape[1]
    out = [
        jax.ShapeDtypeStruct((16, rows // 16, 2 * width), BF16),
        jax.ShapeDtypeStruct((rows, units), F32),
    ]
    return pl.pallas_call(
        rows_kernel,
        grid_spec=pltpu.PrefetchScalarGridSpec(
            num_scalar_prefetch=1,
            grid=(1,),
            in_specs=[
                whole(normed.shape),
                pl.BlockSpec((rows, units), lambda i, at: (at[5], 0)),
                whole(encoder.shape),
            ]
            + [whole(parts[0].shape)] * 8,
            out_specs=[whole(o.shape) for o in out],
            scratch_shapes=[
                pltpu.VMEM((width, units), BF16),
                pltpu.VMEM((tokens, width), BF16),
                pltpu.VMEM((rows, 2 * width), F32),
            ],
        ),
        out_shape=out,
        compiler_params=pltpu.CompilerParams(vmem_limit_bytes=SMALL),
        cost_estimate=pl.CostEstimate(
            flops=2 * rows * width * (tokens + 2 * units),
            bytes_accessed=2 * rows * (tokens + 3 * units),
            transcendentals=0,
        ),
    )(at, normed, w_up, encoder, *parts, *others)


def on_device(tokens, gain, encoder, w_up, w_down, cotangent):
    rows, width = encoder.shape
    own = rows // 16
    dp_at = lax.axis_index("dp")
    mp_at = lax.axis_index("mp")
    core, x, far = dp_at % 2, (dp_at // 2) % 4, dp_at // 8

    z, y = mp_at // 4, mp_at % 4
    tie = lax.optimization_barrier

    other = send(encoder, "dp", step_far)
    as_float = tokens.astype(F32)
    center = as_float - jnp.mean(as_float, axis=1, keepdims=True)
    inv_std = lax.rsqrt(jnp.mean(center * center, axis=1, keepdims=True) + 1e-06)
    unit = center * inv_std
    normed = (unit * gain).astype(BF16)
    spread = normed.reshape(-1, 2, 4, 2, rows).transpose(3, 0, 2, 1, 4).reshape(2, -1, 8 * rows)
    mine, theirs = pick(spread, core, 0), pick(spread, 1 - core, 0)
    other, normed, late_cotangent = tie((other, normed, cotangent))
    parts = gather_parts(jnp.stack(pair_in_order(encoder, other, far)), "dp", step_x)
    line = gather_parts(late_cotangent, "mp", step_z)
    blocks = normed.reshape(-1, 2, 4, 2, rows).transpose(3, 2, 1, 0, 4)
    got = send(pick(blocks, 1 - core, 0), "dp", step_core)
    along = in_order(parts, x).reshape(8 * rows, width)
    along, line, got = tie((along, jnp.concatenate(line), got))
    across = send(along, "dp", step_core)
    after = send(line, "mp", step_y(-1))
    before = send(line, "mp", step_y(1))
    code_rows = jnp.dot(mine, along, preferred_element_type=F32)
    code_rows += jnp.dot(theirs, across, preferred_element_type=F32)
    code_rows = code_rows.astype(BF16)
    all_codes = gather_codes(code_rows)
    blocks = jnp.stack([pick(blocks, core, 0), got], axis=2)
    got = [send(pick(blocks, (x + k) % 4, 0), "dp", step_x(k)) for k in (1, 2, 3)]
    at = jnp.stack([z, y, core, x, far, dp_at]).astype(jnp.int32)
    tied_up = tied_call(at, along, across, w_up)
    after, before, tied_up, _, *got = tie((after, before, tied_up, code_rows, *got))
    blocks = jnp.stack([pick(blocks, x, 0), *got], axis=2)
    half = line.shape[0] // 2
    far_a = send(after[:half], "mp", step_y(-1))
    far_b = send(before[half:], "mp", step_y(1))
    got = send(pick(blocks, 1 - far, 0), "dp", step_far)
    all_codes, tied_up, far_a, far_b, got = tie((all_codes, tied_up, far_a, far_b, got))
    normed_cols = jnp.stack([pick(blocks, far, 0), got], axis=2).reshape(-1, rows)
    pieces = (line, after, far_a, far_b, before)
    keep, give, codes_part, inner, inner_give = mlp_call(at, all_codes, tied_up, w_down, pieces)
    sent = send(give, "dp", step_core)
    grad_codes = scatter_codes(codes_part).astype(BF16)
    inner = add(inner, send(inner_give, "dp", step_core)).astype(BF16)
    first, second = [add(keep[2, k], sent[2, k]).astype(BF16) for k in (0, 1)]
    first, second, inner = tie((first, second, inner))
    got_a = send(first, "dp", step_x(1))
    got_b = send(second, "dp", step_x(-1))
    got = [send(inner[k], "dp", step_x(k)) for k in (1, 2, 3)]
    got_a, got_b, grad_codes, *got = tie((got_a, got_b, grad_codes, *got))
    inner = (inner[0].astype(F32) + sum(g.astype(F32) for g in got)).astype(BF16)
    count, cols = inner.shape
    halves = jnp.split(grad_codes, 2)
    mine = jnp.concatenate([inner, jnp.concatenate(halves, axis=1)])
    up = add(keep[1, 1], sent[1, 1]).astype(BF16)
    down = (add(keep[3, 1], sent[3, 1]) + got_b.astype(F32)).astype(BF16)
    up, down, mine = tie((up, down, mine))
    other = send(mine, "dp", step_far)
    up = send(up, "dp", step_x(1))
    down = send(down, "dp", step_x(-1))
    up, down, other = tie((up, down, other))
    inner = add(inner, other[:count]).astype(BF16)
    mine = jnp.concatenate([inner, mine[count:], other[count:]])
    parts = gather_parts(mine, "dp", step_x)
    total = (add(keep[0, 1], sent[0, 1]) + add(up, down)).astype(BF16)
    across_far = send(total, "dp", step_far)
    up = (add(keep[1, 0], sent[1, 0]) + got_a.astype(F32)).astype(BF16)
    down = add(keep[3, 0], sent[3, 0]).astype(BF16)
    up = send(up, "dp", step_x(1))
    down = send(down, "dp", step_x(-1))
    parts = list(tie(tuple(parts)))
    others = [send(p, "dp", step_core) for p in parts]
    both, grad_up = rows_call(at, normed_cols, w_up, encoder, parts, others)
    both, across_far = tie((both, across_far))
    grad_down = add(keep[0, 0], sent[0, 0]) + add(up, down) + across_far.astype(F32)
    both = lax.all_to_all(both, "mp", split_axis=0, concat_axis=0)
    both = jnp.sum(both.astype(F32), axis=0)
    own_encoder = lax.dynamic_slice_in_dim(encoder, mp_at * own, own, 0).astype(F32)
    own_gain = lax.dynamic_slice_in_dim(gain, dp_at * rows + mp_at * own, own, 0)
    grad_encoder = both[:, :width] + both[:, width:]
    grad_gain = jnp.sum(own_encoder * both[:, :width], axis=1) / own_gain
    full_encoder = join_encoder(along, across, core)
    d_normed = jnp.einsum("tc,dc->td", grad_codes, full_encoder, preferred_element_type=F32)
    dx_hat = d_normed * gain
    mean_one = jnp.mean(dx_hat, axis=1, keepdims=True)
    mean_two = jnp.mean(dx_hat * unit, axis=1, keepdims=True)
    grad_tokens = (
        cotangent.astype(F32) + inv_std * (dx_hat - mean_one - unit * mean_two)
    ).astype(BF16)
    return (grad_tokens, grad_up, grad_down, grad_encoder, grad_gain)


def solution(mesh):
    placed = (
        P(("dp", "mp"), None),
        P(),
        P("dp", None),
        P(None, "mp"),
        P(None, "mp"),
        P(("dp", "mp"), None),
    )
    return jax.shard_map(
        on_device,
        mesh=mesh,
        in_specs=placed,
        out_specs=(
            P(("dp", "mp"), None),
            P("dp", "mp"),
            P("dp", "mp"),
            P(("dp", "mp"), None),
            P(("dp", "mp")),
        ),
        check_vma=False,
    )
```

```python
import jax
import jax.numpy as jnp
from jax import lax
from jax.experimental import pallas as pl
from jax.experimental.pallas import tpu as pltpu
from jax.sharding import PartitionSpec as P

F32 = jnp.float32
BF16 = jnp.bfloat16


def step_core(i):
    return i ^ 1


def step_far(i):
    return i ^ 8


def step_x(k):
    return lambda i: (i & 9) | ((((i >> 1) + k) & 3) << 1)


def step_y(k):
    return lambda i: (i & 12) | ((i + k) & 3)


def step_z(k):
    return lambda i: ((((i >> 2) + k) & 3) << 2) | (i & 3)


def send(value, axis, target):
    return lax.ppermute(value, axis, [(i, target(i)) for i in range(16)])


def gather_parts(value, axis, step):
    return [value] + [send(value, axis, step(-k)) for k in (1, 2, 3)]


def in_order(parts, at):
    n = len(parts)
    twice = jnp.stack(parts + parts[:-1])
    return lax.dynamic_slice_in_dim(twice, (n - at) % n, n, 0)


def pair_in_order(mine, other, at):
    first = jnp.where(at == 0, mine, other)
    second = jnp.where(at == 0, other, mine)
    return first, second


def pick(value, at, axis):
    return lax.dynamic_index_in_dim(value, at, axis, keepdims=False)


def gelu_parts(pre_act):
    cdf_part = 0.5 * (1.0 + lax.erf(pre_act * 0.7071067811865476))
    density = jnp.exp(-0.5 * pre_act * pre_act) * 0.3989422804014327
    return (pre_act * cdf_part, cdf_part + pre_act * density)


def add(a, b):
    return a.astype(F32) + b.astype(F32)


def join_encoder(along, across, core):
    width = along.shape[1]
    full = jnp.stack(pair_in_order(along, across, core)).reshape(2, 4, 2, -1, width)
    return full.transpose(2, 1, 0, 3, 4).reshape(-1, width)


def gather_codes(code_rows):
    count, width = code_rows.shape
    return lax.all_to_all(
        jnp.broadcast_to(code_rows, (16, count, width)), "mp", split_axis=0, concat_axis=0
    )


VMEM = 58 * 1024 * 1024
SMALL = 16 * 1024 * 1024


def token_block(k, at):
    return ((at[0] + k % 4) % 4) * 4 + (at[1] + k // 4) % 4


def fill_rows(at, codes, rows):
    count = codes.shape[1]
    for k in range(16):
        rows[k * count : (k + 1) * count, :] = codes[token_block(k, at)]


def row_copies(pieces, rows, sems):
    copies, start = [], 0
    for k, piece in enumerate(pieces):
        count = piece.shape[0]
        copies.append(
            pltpu.make_async_copy(piece, rows.at[pl.ds(start, count), :], sems.at[k])
        )
        start += count
    return copies


def whole(shape):
    return pl.BlockSpec(shape, lambda i, at: (0,) * len(shape))


def mlp_kernel(at, codes, tied, w_down, *refs):
    pieces, (keep, give, codes_part, inner, inner_give) = refs[:5], refs[5:10]
    rows, hidden, slope, total, upstream, weights, sems = refs[10:]
    step = pl.program_id(0)
    span = 2 * keep.shape[2]
    here = pl.ds(pl.multiple_of(step * span, span), span)

    def weight_copy(k):
        part = pl.ds(pl.multiple_of(k * span, span), span)
        return pltpu.make_async_copy(w_down.at[part, :], weights.at[part, :], sems.at[5 + k])

    @pl.when(step == 0)
    def _():
        copies = row_copies(pieces, upstream, sems)
        for c in copies:
            c.start()
        for k in range(2):
            weight_copy(k).start()
        fill_rows(at, codes, rows)
        pre_act = jnp.dot(rows[...], tied[...], preferred_element_type=F32)
        value, grade = gelu_parts(pre_act)
        hidden[...] = value.astype(BF16)
        slope[...] = grade
        total[...] = jnp.zeros_like(total)
        for c in copies:
            c.wait()
        for k in range(2, 8):
            weight_copy(k).start()

    weight_copy(step).wait()
    part = upstream[:, here]
    total[...] += jnp.dot(part, weights[here, :], preferred_element_type=F32)
    term = lax.dot_general(
        part, hidden[...], (((0,), (0,)), ((), ())), preferred_element_type=F32
    ).astype(BF16)
    half = term.shape[0] // 2
    first, second = term[:half], term[half:]

    @pl.when(at[2] == 0)
    def _():
        keep[0, 0] = first
        give[0, 0] = second

    @pl.when(at[2] != 0)
    def _():
        keep[0, 0] = second
        give[0, 0] = first

    @pl.when(step == 7)
    def _():
        d_act = (total[...] * slope[...]).astype(BF16)
        back = lax.dot_general(
            d_act, tied[...], (((1,), (1,)), ((), ())), preferred_element_type=F32
        ).astype(BF16)
        count = codes.shape[1]
        for k in range(16):
            codes_part[token_block(k, at)] = back[k * count : (k + 1) * count, :]
        outer = lax.dot_general(
            rows[...], d_act, (((0,), (0,)), ((), ())), preferred_element_type=F32
        ).astype(BF16)
        piece = outer.shape[0] // 8
        lower = at[2] == 0
        for k in range(4):
            first = outer[k * piece : (k + 1) * piece, :]
            second = outer[(k + 4) * piece : (k + 5) * piece, :]
            inner[(k + 4 - at[3]) % 4] = jnp.where(lower, first, second)
            inner_give[(k + 4 - at[3]) % 4] = jnp.where(lower, second, first)


def mlp_call(at, codes, tied, w_down, pieces):
    width, units = tied.shape
    tokens = codes.shape[0] * codes.shape[1]
    features = w_down.shape[0]
    span = features // 8

    def place(i, at):
        return ((i % 4 + 4 - at[3]) % 4, (i // 4 + at[4]) % 2, 0, 0)

    out = [jax.ShapeDtypeStruct((4, 2, span // 2, units), BF16)] * 2
    out += [
        jax.ShapeDtypeStruct(codes.shape, BF16),
        jax.ShapeDtypeStruct((4, width // 8, units), BF16),
        jax.ShapeDtypeStruct((4, width // 8, units), BF16),
    ]
    return pl.pallas_call(
        mlp_kernel,
        grid_spec=pltpu.PrefetchScalarGridSpec(
            num_scalar_prefetch=1,
            grid=(8,),
            in_specs=[whole(codes.shape), whole(tied.shape)]
            + [pl.BlockSpec(memory_space=pltpu.HBM)]
            + [pl.BlockSpec(memory_space=pltpu.HBM)] * 5,
            out_specs=[pl.BlockSpec((1, 1, span // 2, units), place)] * 2
            + [whole(o.shape) for o in out[2:]],
            scratch_shapes=[
                pltpu.VMEM((tokens, width), BF16),
                pltpu.VMEM((tokens, units), BF16),
                pltpu.VMEM((tokens, units), F32),
                pltpu.VMEM((tokens, units), F32),
                pltpu.VMEM((tokens, features), BF16),
                pltpu.VMEM((features, units), BF16),
                pltpu.SemaphoreType.DMA((13,)),
            ],
        ),
        out_shape=out,
        compiler_params=pltpu.CompilerParams(vmem_limit_bytes=VMEM),
        cost_estimate=pl.CostEstimate(
            flops=4 * tokens * units * (features + width),
            bytes_accessed=2 * (3 * features * units + tokens * features),
            transcendentals=2 * tokens * units,
        ),
    )(at, codes, tied, w_down, *pieces)


def tied_kernel(at, along, across, w_up, out, total):
    step = pl.program_id(0)
    mine, other = along[0], across[0]
    lower = at[2] == 0
    block = jnp.concatenate(
        [jnp.where(lower, mine, other), jnp.where(lower, other, mine)], axis=0
    )
    part = lax.dot_general(
        block, w_up[...], (((0,), (0,)), ((), ())), preferred_element_type=F32
    )

    @pl.when(step == 0)
    def _():
        total[...] = part

    @pl.when(step != 0)
    def _():
        total[...] += part

    @pl.when(step == 7)
    def _():
        out[...] = total[...].astype(BF16)


def tied_call(at, along, across, w_up):
    rows, width = along.shape[0] // 8, along.shape[1]
    units = w_up.shape[1]
    block = pl.BlockSpec((1, rows, width), lambda i, at: (i, 0, 0))
    return pl.pallas_call(
        tied_kernel,
        grid_spec=pltpu.PrefetchScalarGridSpec(
            num_scalar_prefetch=1,
            grid=(8,),
            in_specs=[
                block,
                block,
                pl.BlockSpec((2 * rows, units), lambda i, at: (i % 2 * 4 + i // 2, 0)),
            ],
            out_specs=whole((width, units)),
            scratch_shapes=[pltpu.VMEM((width, units), F32)],
        ),
        out_shape=jax.ShapeDtypeStruct((width, units), BF16),
        compiler_params=pltpu.CompilerParams(vmem_limit_bytes=SMALL),
        cost_estimate=pl.CostEstimate(
            flops=32 * rows * width * units, bytes_accessed=64 * rows * units, transcendentals=0
        ),
    )(at, along.reshape(8, rows, width), across.reshape(8, rows, width), w_up)


def rows_kernel(at, normed, w_up, encoder, *refs):
    parts, (both, grad_up, inner, codes, sums) = (refs[:4], refs[4:8]), refs[8:]
    width = encoder.shape[1]
    units = w_up.shape[1]
    count = inner.shape[0] // 8
    for c in range(2):
        for k in range(4):
            part = parts[c][k]
            place = ((at[2] + c) % 2 * 4 + (at[3] + k) % 4) * count
            inner[pl.ds(pl.multiple_of(place, count), count), :] = part[:count, :]
            place = (c * 4 + (4 - k) % 4) * 64
            for j in range(4):
                codes[place + 16 * j : place + 16 * (j + 1), :] = part[
                    count + 16 * (j // 2) : count + 16 * (j // 2 + 1),
                    width * (j % 2) : width * (j % 2 + 1),
                ]
    sums[:, :width] = lax.dot_general(
        normed[...], codes[...], (((0,), (0,)), ((), ())), preferred_element_type=F32
    )
    sums[:, width:] = lax.dot_general(
        w_up[...], inner[...], (((1,), (1,)), ((), ())), preferred_element_type=F32
    )
    own = both.shape[1]
    for k in range(16):
        both[k] = sums[k * own : (k + 1) * own, :].astype(BF16)
    grad_up[...] = jnp.dot(encoder[...], inner[...], preferred_element_type=F32)


def rows_call(at, normed, w_up, encoder, parts, others):
    tokens, rows = normed.shape
    width, units = encoder.shape[1], w_up.shape[1]
    out = [
        jax.ShapeDtypeStruct((16, rows // 16, 2 * width), BF16),
        jax.ShapeDtypeStruct((rows, units), F32),
    ]
    return pl.pallas_call(
        rows_kernel,
        grid_spec=pltpu.PrefetchScalarGridSpec(
            num_scalar_prefetch=1,
            grid=(1,),
            in_specs=[
                whole(normed.shape),
                pl.BlockSpec((rows, units), lambda i, at: (at[5], 0)),
                whole(encoder.shape),
            ]
            + [whole(parts[0].shape)] * 8,
            out_specs=[whole(o.shape) for o in out],
            scratch_shapes=[
                pltpu.VMEM((width, units), BF16),
                pltpu.VMEM((tokens, width), BF16),
                pltpu.VMEM((rows, 2 * width), F32),
            ],
        ),
        out_shape=out,
        compiler_params=pltpu.CompilerParams(vmem_limit_bytes=SMALL),
        cost_estimate=pl.CostEstimate(
            flops=2 * rows * width * (tokens + 2 * units),
            bytes_accessed=2 * rows * (tokens + 3 * units),
            transcendentals=0,
        ),
    )(at, normed, w_up, encoder, *parts, *others)


def on_device(tokens, gain, encoder, w_up, w_down, cotangent):
    rows, width = encoder.shape
    own = rows // 16
    dp_at = lax.axis_index("dp")
    mp_at = lax.axis_index("mp")
    core, x, far = dp_at % 2, (dp_at // 2) % 4, dp_at // 8

    z, y = mp_at // 4, mp_at % 4
    tie = lax.optimization_barrier

    other = send(encoder, "dp", step_far)
    as_float = tokens.astype(F32)
    center = as_float - jnp.mean(as_float, axis=1, keepdims=True)
    inv_std = lax.rsqrt(jnp.mean(center * center, axis=1, keepdims=True) + 1e-06)
    unit = center * inv_std
    normed = (unit * gain).astype(BF16)
    spread = normed.reshape(-1, 2, 4, 2, rows).transpose(3, 0, 2, 1, 4).reshape(2, -1, 8 * rows)
    mine, theirs = pick(spread, core, 0), pick(spread, 1 - core, 0)
    other, normed, late_cotangent = tie((other, normed, cotangent))
    parts = gather_parts(jnp.stack(pair_in_order(encoder, other, far)), "dp", step_x)
    line = gather_parts(late_cotangent, "mp", step_z)
    blocks = normed.reshape(-1, 2, 4, 2, rows).transpose(3, 2, 1, 0, 4)
    got = send(pick(blocks, 1 - core, 0), "dp", step_core)
    along = in_order(parts, x).reshape(8 * rows, width)
    along, line, got = tie((along, jnp.concatenate(line), got))
    across = send(along, "dp", step_core)
    after = send(line, "mp", step_y(-1))
    before = send(line, "mp", step_y(1))
    code_rows = jnp.dot(mine, along, preferred_element_type=F32)
    code_rows += jnp.dot(theirs, across, preferred_element_type=F32)
    code_rows = code_rows.astype(BF16)
    all_codes = gather_codes(code_rows)
    blocks = jnp.stack([pick(blocks, core, 0), got], axis=2)
    got = [send(pick(blocks, (x + k) % 4, 0), "dp", step_x(k)) for k in (1, 2, 3)]
    at = jnp.stack([z, y, core, x, far, dp_at]).astype(jnp.int32)
    tied_up = tied_call(at, along, across, w_up)
    after, before, tied_up, _, *got = tie((after, before, tied_up, code_rows, *got))
    blocks = jnp.stack([pick(blocks, x, 0), *got], axis=2)
    half = line.shape[0] // 2
    far_a = send(after[:half], "mp", step_y(-1))
    far_b = send(before[half:], "mp", step_y(1))
    got = send(pick(blocks, 1 - far, 0), "dp", step_far)
    all_codes, tied_up, far_a, far_b, got = tie((all_codes, tied_up, far_a, far_b, got))
    normed_cols = jnp.stack([pick(blocks, far, 0), got], axis=2).reshape(-1, rows)
    pieces = (line, after, far_a, far_b, before)
    keep, give, codes_part, inner, inner_give = mlp_call(at, all_codes, tied_up, w_down, pieces)
    sent = send(give, "dp", step_core)
    grad_codes = lax.all_to_all(codes_part, "mp", split_axis=0, concat_axis=0)
    inner = add(inner, send(inner_give, "dp", step_core)).astype(BF16)
    first, second = [add(keep[2, k], sent[2, k]).astype(BF16) for k in (0, 1)]
    first, second, inner, keep, sent = tie((first, second, inner, keep, sent))
    got_a = send(first, "dp", step_x(1))
    got_b = send(second, "dp", step_x(-1))
    got = [send(inner[k], "dp", step_x(k)) for k in (1, 2, 3)]
    got_a, got_b, grad_codes, *got = tie((got_a, got_b, grad_codes, *got))
    grad_codes = jnp.sum(grad_codes.astype(F32), axis=0).astype(BF16)
    inner = (inner[0].astype(F32) + sum(g.astype(F32) for g in got)).astype(BF16)
    count, cols = inner.shape
    halves = jnp.split(grad_codes, 2)
    mine = jnp.concatenate([inner, jnp.concatenate(halves, axis=1)])
    up = add(keep[1, 1], sent[1, 1]).astype(BF16)
    down = (add(keep[3, 1], sent[3, 1]) + got_b.astype(F32)).astype(BF16)
    up, down, mine = tie((up, down, mine))
    other = send(mine, "dp", step_far)
    up = send(up, "dp", step_x(1))
    down = send(down, "dp", step_x(-1))
    up, down, other = tie((up, down, other))
    inner = add(inner, other[:count]).astype(BF16)
    mine = jnp.concatenate([inner, mine[count:], other[count:]])
    parts = gather_parts(mine, "dp", step_x)
    total = (add(keep[0, 1], sent[0, 1]) + add(up, down)).astype(BF16)
    across_far = send(total, "dp", step_far)
    up = (add(keep[1, 0], sent[1, 0]) + got_a.astype(F32)).astype(BF16)
    down = add(keep[3, 0], sent[3, 0]).astype(BF16)
    up = send(up, "dp", step_x(1))
    down = send(down, "dp", step_x(-1))
    parts = list(tie(tuple(parts)))
    others = [send(p, "dp", step_core) for p in parts]
    both, grad_up = rows_call(at, normed_cols, w_up, encoder, parts, others)
    both, across_far = tie((both, across_far))
    grad_down = add(keep[0, 0], sent[0, 0]) + add(up, down) + across_far.astype(F32)
    both = lax.all_to_all(both, "mp", split_axis=0, concat_axis=0)
    both = jnp.sum(both.astype(F32), axis=0)
    own_encoder = lax.dynamic_slice_in_dim(encoder, mp_at * own, own, 0).astype(F32)
    own_gain = lax.dynamic_slice_in_dim(gain, dp_at * rows + mp_at * own, own, 0)
    grad_encoder = both[:, :width] + both[:, width:]
    grad_gain = jnp.sum(own_encoder * both[:, :width], axis=1) / own_gain
    full_encoder = join_encoder(along, across, core)
    d_normed = jnp.einsum("tc,dc->td", grad_codes, full_encoder, preferred_element_type=F32)
    dx_hat = d_normed * gain
    mean_one = jnp.mean(dx_hat, axis=1, keepdims=True)
    mean_two = jnp.mean(dx_hat * unit, axis=1, keepdims=True)
    grad_tokens = (
        cotangent.astype(F32) + inv_std * (dx_hat - mean_one - unit * mean_two)
    ).astype(BF16)
    return (grad_tokens, grad_up, grad_down, grad_encoder, grad_gain)


def solution(mesh):
    placed = (
        P(("dp", "mp"), None),
        P(),
        P("dp", None),
        P(None, "mp"),
        P(None, "mp"),
        P(("dp", "mp"), None),
    )
    return jax.shard_map(
        on_device,
        mesh=mesh,
        in_specs=placed,
        out_specs=(
            P(("dp", "mp"), None),
            P("dp", "mp"),
            P("dp", "mp"),
            P(("dp", "mp"), None),
            P(("dp", "mp")),
        ),
        check_vma=False,
    )
```
